768 devices in a mesh: rows: 96 (over y_lo, z, core), blk: 8 (over y_hi, x).
Axes of the slice: x: 4, y: 8 (y_hi: 2, y_lo: 4; y = y_hi * 4 + y_lo), z: 12, core: 2. Of those that a mesh axis runs over, the one named last changes fastest.
Arguments:
- features: bfloat16 [196608, 256], P(('rows', 'blk')), may hold values from -32 to 32
- w_self: bfloat16 [256, 172], replicated, may hold values from -1 to 1
- w_neigh: bfloat16 [256, 172], replicated, may hold values from -0.375 to 0.375
- block_cols: int32 [1536, 6], P(('rows', 'blk')), may hold values from 0 to 15
- block_count: int32 [1536], P(('rows', 'blk')), may hold values from 1 to 6, as said below
- block_values: bfloat16 [1536, 6, 128, 128], P(('rows', 'blk')), may hold values from 0.049804688 to 1
- labels: int32 [196608], P(('rows', 'blk')), may hold values from 0 to 171
Outputs:
- loss: float32 [], replicated
- grad_self: float32 [256, 172], replicated
- grad_neigh: float32 [256, 172], replicated
- grad_features: bfloat16 [196608, 256], P(('rows', 'blk'))
The draws below stay inside these ranges and needn't reach their ends.
Inputs may be any that keep to these rules, and one draw needn't show every extreme that they name: `block_count`: each row group's row blocks include one with exactly 6 used slots.
All inputs are finite; a program needn't handle non-finite values.
Results may differ from the reference program's by a relative error of at most 0.01.
Values may be sent and summed in bfloat16 or wider, within the bound.
No kernel may reach another device: no remote copies, remote signals or barrier semaphores. Data moves between devices by JAX's collectives and lax.ppermute only.
A program may use at most 64 MiB of HBM per device.

```python
import math
import jax
import jax.numpy as jnp
from jax import lax

F = 256
C = 172
BS = 128
MAXNZ = 6
ROW_BLOCKS = 1536
GROUP_BLOCKS = 16
NODES = 196608


def draw_features(key, part):
    key = jax.random.fold_in(key, 5)
    return jnp.clip(jax.random.normal(key, (NODES, F), jnp.float32), -6.0, 6.0).astype(jnp.bfloat16)


def draw_w_self(key, part):
    key = jax.random.fold_in(key, 7)
    base = jnp.clip(jax.random.normal(key, (F, C), jnp.float32), -5.0, 5.0) * F ** (-0.5)
    return base.astype(jnp.bfloat16)


def draw_block_count(key, part):
    key = jax.random.fold_in(key, 11)
    keys = jax.random.split(key, 2)
    counts = jax.random.randint(keys[0], (ROW_BLOCKS,), 1, MAXNZ + 1)
    groups = ROW_BLOCKS // GROUP_BLOCKS
    position = jax.random.randint(keys[1], (groups,), 0, GROUP_BLOCKS)
    full = (jnp.arange(GROUP_BLOCKS)[None, :] == position[:, None]).reshape(ROW_BLOCKS)
    return jnp.where(full, MAXNZ, counts).astype(jnp.int32)


def set_ends(drawn, stream_key, low, high):
    longest = drawn.shape.index(max(drawn.shape))
    spots = []
    for shift in (0, 1):
        where = [jax.random.randint(jax.random.fold_in(stream_key, axis), (), 0, length) for axis, length in enumerate(drawn.shape)]
        where[longest] = (where[longest] + shift) % drawn.shape[longest]
        spots.append(tuple(where))
    return drawn.at[spots[0]].set(low).at[spots[1]].set(high)


def shard_levels(rng, dims, shards, low, high):
    def one(dim, parts):
        heights = jax.random.uniform(jax.random.fold_in(jax.random.fold_in(rng, 6), dim), (parts,), jnp.float32, low / len(shards), high / len(shards))
        return jnp.repeat(jnp.exp(heights), dims[dim] // parts).reshape((-1,) + (1,) * (len(dims) - dim - 1))

    factor_of = one(*shards[0])
    for cut in shards[1:]:
        factor_of = factor_of * one(*cut)
    return factor_of


def gaussian(own_key, extent, deviation, reach, dtype=jnp.bfloat16):
    return jnp.clip(deviation * jax.random.normal(own_key, extent, jnp.float32), -reach, reach).astype(dtype)


def setup_inputs(seed: int = 0) -> dict:
    splits = jax.random.split(jax.random.key(seed), 8)
    features = draw_features(jax.random.fold_in(splits[7], 71), 0)
    w_self = draw_w_self(jax.random.fold_in(splits[7], 71), 0)
    w_neigh = gaussian(splits[2], (F, C), F ** -0.5, 0.375)
    block_cols = set_ends(jax.random.randint(splits[3], (ROW_BLOCKS, MAXNZ), 0, GROUP_BLOCKS), jax.random.fold_in(splits[3], 1), 0, GROUP_BLOCKS - 1).astype(jnp.int32)
    block_count = draw_block_count(jax.random.fold_in(splits[7], 71), 0)
    block_values = jnp.clip(jnp.exp(math.log(1.0) - 2.9996462 * jax.random.uniform(splits[5], (ROW_BLOCKS, MAXNZ, BS, BS), jnp.float32) ** shard_levels(splits[5], (ROW_BLOCKS, MAXNZ, BS, BS), ((0, 768),), -0.2, 0.2)), 0.049804688, 1.0).astype(jnp.bfloat16)
    labels = set_ends(jax.random.randint(splits[6], (NODES,), 0, C), jax.random.fold_in(splits[6], 1), 0, C - 1).astype(jnp.int32)
    return {"features": features, "w_self": w_self, "w_neigh": w_neigh, "block_cols": block_cols, "block_count": block_count, "block_values": block_values, "labels": labels}


def group_matrix(cols, counts, values):
    used = jnp.arange(MAXNZ)[None, :] < counts[:, None]
    pick = ((cols[:, :, None] == jnp.arange(GROUP_BLOCKS)[None, None, :]) & used[:, :, None]).astype(jnp.float32)
    dense = jnp.einsum('bsc,bsij->bicj', pick, values.astype(jnp.float32), precision=lax.Precision.HIGHEST)
    dense = dense.reshape(GROUP_BLOCKS * BS, GROUP_BLOCKS * BS)
    degree = jnp.einsum('bs,bsij->bi', used.astype(jnp.float32), values.astype(jnp.float32), precision=lax.Precision.HIGHEST)
    return dense, degree.reshape(GROUP_BLOCKS * BS)


def reference(features, w_self, w_neigh, block_cols, block_count, block_values, labels):
    groups = ROW_BLOCKS // GROUP_BLOCKS
    span = GROUP_BLOCKS * BS
    cols_g = block_cols.reshape(groups, GROUP_BLOCKS, MAXNZ)
    count_g = block_count.reshape(groups, GROUP_BLOCKS)
    vals_g = block_values.reshape(groups, GROUP_BLOCKS, MAXNZ, BS, BS)
    feat_g = features.reshape(groups, span, F)

    def forward(items):
        cols, counts, values, feats = items
        dense, degree = group_matrix(cols, counts, values)
        total = jnp.dot(dense, feats.astype(jnp.float32), precision=lax.Precision.HIGHEST)
        return (total / degree[:, None]).astype(jnp.bfloat16), degree

    aggregate, degree = lax.map(forward, (cols_g, count_g, vals_g, feat_g))
    aggregate = aggregate.reshape(NODES, F)
    degree = degree.reshape(NODES)
    logits = jnp.dot(features, w_self, preferred_element_type=jnp.float32) + jnp.dot(aggregate, w_neigh, preferred_element_type=jnp.float32)
    top = jnp.max(logits, axis=1, keepdims=True)
    shifted = jnp.exp(logits - top)
    total_exp = jnp.sum(shifted, axis=1, keepdims=True)
    lse = jnp.log(total_exp) + top
    target = (jnp.arange(C)[None, :] == labels[:, None])
    picked = jnp.sum(jnp.where(target, logits, 0.0), axis=1)
    loss = jnp.sum(lse[:, 0] - picked) / NODES
    dlogits = (shifted / total_exp - target.astype(jnp.float32)).astype(jnp.bfloat16)
    factor = float(NODES) ** -0.5
    grad_self = jnp.dot(features.T, dlogits, preferred_element_type=jnp.float32) * factor
    grad_neigh = jnp.dot(aggregate.T, dlogits, preferred_element_type=jnp.float32) * factor
    scaled = (jnp.dot(dlogits, w_neigh.T, preferred_element_type=jnp.float32) / degree[:, None]).astype(jnp.bfloat16)
    scaled_g = scaled.reshape(groups, span, F)

    def backward(items):
        cols, counts, values, rowgrad = items
        dense, unused = group_matrix(cols, counts, values)
        return jnp.dot(dense.T, rowgrad.astype(jnp.float32), precision=lax.Precision.HIGHEST)

    partial_sum = lax.map(backward, (cols_g, count_g, vals_g, scaled_g)).reshape(NODES, F)
    grad_features = (jnp.dot(dlogits, w_self.T, preferred_element_type=jnp.float32) + partial_sum).astype(jnp.bfloat16)
    return loss, grad_self, grad_neigh, grad_features
```

```python
import functools

import jax
import jax.numpy as jnp
from jax import lax
from jax.experimental import pallas as pl
from jax.experimental.pallas import tpu as pltpu
from jax.sharding import Mesh, PartitionSpec as P

AXES = ("y_lo", "z", "core", "y_hi", "x")
SIZES = (4, 12, 2, 2, 4)
NEAR = ("y_lo", "y_hi", "x")
FAR = ("z", "core")
N_NEAR, N_FAR = 32, 24
BS = 128
F = 256
C = 172
CP = 176
PIECE = 24
LOSS_ROW = C
ANY = pl.BlockSpec(memory_space=pl.ANY)
SMEM = pl.BlockSpec(memory_space=pltpu.SMEM)
VMEM = pl.BlockSpec(memory_space=pltpu.VMEM)
PARAMS = pltpu.CompilerParams(vmem_limit_bytes=40 * 2**20)


def split_three(value):
    high = value.astype(jnp.bfloat16).astype(jnp.float32)
    rest = value - high
    mid = rest.astype(jnp.bfloat16).astype(jnp.float32)
    return high, mid, rest - mid


def put_copies(source, out, start, sems):
    rows = pl.ds(start, source.shape[0])
    copies = [pltpu.make_async_copy(source, out.at[i, rows], sems.at[i]) for i in range(out.shape[0])]
    for copy in copies:
        copy.start()
    for copy in copies:
        copy.wait()


def copies_kernel(source, out, sems):
    put_copies(source, out, 0, sems)


def layer_kernel(
    table, feats_all, feats, w_self_t, w_neigh_t, w_self, values, labels,
    grads, keep, send, own, terms,
):
    nblocks, slots = values.shape[0], values.shape[1]
    cols = [[table[b * slots + s] for s in range(slots)] for b in range(nblocks)]
    counts = [table[nblocks * slots + b] for b in range(nblocks)]
    my_half, my_x = table[nblocks * (slots + 1)], table[nblocks * (slots + 1) + 1]

    def home(col):
        return (col // 2) % 4, (col // 8) ^ my_half, col % 2

    def start_row(col):
        owner_x, _, second = home(col)
        return pl.multiple_of((owner_x * 4 + (col // 8) * 2 + second) * BS, BS)

    live = []
    degree_col, degree_row, summed = [], [], []
    for b in range(nblocks):
        row = []
        total = None
        for s in range(slots):
            used = jnp.where(s < counts[b], 1.0, 0.0).astype(jnp.float32)
            block = values[b, s] * jnp.full((BS, BS), used, jnp.float32).astype(jnp.bfloat16)
            row.append(block)
            wide = block.astype(jnp.float32)
            total = wide if total is None else total + wide
        live.append(row)
        degree = jnp.sum(total, axis=1, keepdims=True)
        degree_col.append(degree)
        degree_row.append(jnp.broadcast_to(degree, (BS, BS)).T[0:1, :])
        picked = jnp.concatenate(
            [feats_all[pl.ds(start_row(cols[b][s]), BS), :] for s in range(slots)], axis=0
        )
        summed.append(
            jnp.dot(jnp.concatenate(row, axis=1), picked, preferred_element_type=jnp.float32) / degree
        )
    aggregate = jnp.concatenate(summed, axis=0).astype(jnp.bfloat16)
    degrees = jnp.concatenate(degree_row, axis=1)
    own_feats = feats[...]
    nt = (((1,), (1,)), ((), ()))
    logits = lax.dot_general(
        w_self_t[...], own_feats, nt, preferred_element_type=jnp.float32
    ) + lax.dot_general(w_neigh_t[...], aggregate, nt, preferred_element_type=jnp.float32)
    classes = lax.broadcasted_iota(jnp.int32, logits.shape, 0)
    real = classes < C
    top = jnp.max(jnp.where(real, logits, -3.0e38), axis=0, keepdims=True)
    shifted = jnp.where(real, jnp.exp(jnp.where(real, logits - top, 0.0)), 0.0)
    total_exp = jnp.sum(shifted, axis=0, keepdims=True)
    target = classes == labels[0:1, :]
    picked_logit = jnp.sum(jnp.where(target, logits, 0.0), axis=0, keepdims=True)
    lse = jnp.log(total_exp) + top
    loss = jnp.sum(lse - picked_logit, axis=1, keepdims=True)
    dlogits = (shifted / total_exp - jnp.where(target, 1.0, 0.0)).astype(jnp.bfloat16)

    high, mid, low = split_three(loss)
    both = (own_feats, aggregate)
    rows = lax.broadcasted_iota(jnp.int32, (CP, BS), 0)
    for q in range(4):
        side = both[q // 2][:, (q % 2) * BS : (q % 2 + 1) * BS]
        part = jnp.dot(dlogits, side, preferred_element_type=jnp.float32)
        if q == 0:
            part = jnp.where(rows == LOSS_ROW, high, part)
            part = jnp.where(rows == LOSS_ROW + 1, mid, part)
            part = jnp.where(rows == LOSS_ROW + 2, low, part)
        grads[q * CP : (q + 1) * CP, :] = part.astype(jnp.bfloat16)
    pad = grads.shape[0] - 4 * CP
    grads[4 * CP :, :] = jnp.zeros((pad, BS), jnp.bfloat16)

    own[...] = jnp.dot(w_self[...], dlogits, preferred_element_type=jnp.float32)
    scaled = (dlogits.astype(jnp.float32) / degrees).astype(jnp.bfloat16)
    terms[...] = jnp.zeros_like(terms)
    for b in range(nblocks):
        mine = scaled[:, b * BS : (b + 1) * BS]
        for s in range(slots):
            term = jnp.dot(mine, live[b][s], preferred_element_type=jnp.float32)
            owner_x, across, second = home(cols[b][s])
            delta = owner_x ^ my_x
            late = delta // 2
            early = (delta % 2) ^ late
            terms[early * 8 + late * 4 + across * 2 + second] += term
    keep[...] = terms[0:8]
    send[...] = terms[8:16].astype(jnp.bfloat16)


def halve_kernel(kept, came, keep, send):
    half = kept.shape[0] // 2
    keep[...] = kept[0:half] + came[0:half].astype(jnp.float32)
    send[...] = (kept[half:] + came[half:].astype(jnp.float32)).astype(jnp.bfloat16)


def features_kernel(kept, came, own, w_neigh, out):
    for r in range(2):
        scattered = (kept[r] + came[r].astype(jnp.float32)).astype(jnp.bfloat16)
        total = own[:, r * BS : (r + 1) * BS] + jnp.dot(
            w_neigh[...], scattered, preferred_element_type=jnp.float32
        )
        out[r * BS : (r + 1) * BS, :] = total.T.astype(jnp.bfloat16)


def spread(total, loss_here, out):
    rows = lax.broadcasted_iota(jnp.int32, total.shape, 0)
    here = LOSS_ROW % PIECE
    carries = (rows >= here) & (rows < here + 3)
    loss = jnp.sum(jnp.where(carries, total, 0.0), axis=0, keepdims=True)
    high, mid, low = split_three(loss)
    fixed = jnp.where(rows == here, high, jnp.where(rows == here + 1, mid, low))
    use = carries & (jnp.full(total.shape, loss_here[0], jnp.int32) == 1)
    out[...] = jnp.broadcast_to(jnp.where(use, fixed, total).astype(jnp.bfloat16)[None], out.shape)


def piece_kernel(loss_here, pieces, after, out):
    spread(jnp.sum(pieces[...].astype(jnp.float32), axis=0), loss_here, out)


def grads_kernel(nodes_all, pieces, loss, grad_self, grad_neigh):
    factor = float(nodes_all) ** (-0.5)
    outs = (grad_self, grad_neigh)
    for q in range(4):
        part = pieces[q * CP : (q + 1) * CP, :].astype(jnp.float32)
        if q == 0:
            carried = part[LOSS_ROW - 4 : CP, :]
            rows = lax.broadcasted_iota(jnp.int32, carried.shape, 0)
            lanes = lax.broadcasted_iota(jnp.int32, carried.shape, 1)
            use = (rows >= 4) & (rows < 7) & (lanes == 0)
            loss[0, 0] = jnp.sum(jnp.where(use, carried, 0.0)) / nodes_all
        outs[q // 2][:, (q % 2) * BS : (q % 2 + 1) * BS] = part[:C] * factor


def call(kernel, outs, in_specs, out_specs=None, scratch=(), aliases=None):
    shapes = [jax.ShapeDtypeStruct(shape, dtype) for shape, dtype in outs]
    return pl.pallas_call(
        kernel,
        out_shape=shapes,
        in_specs=in_specs,
        out_specs=out_specs or [VMEM] * len(shapes),
        scratch_shapes=list(scratch),
        input_output_aliases=aliases or {},
        compiler_params=PARAMS,
    )


def exchange(rows, axes):
    return lax.all_to_all(rows, axes, 0, 0, tiled=True)


def per_device(features, w_self, w_neigh, block_cols, block_count, block_values, labels):
    bf16, f32 = jnp.bfloat16, jnp.float32
    own_rows = features.shape[0]
    nodes_all = own_rows * 768
    y_lo, y_hi, x = (lax.axis_index(a) for a in NEAR)
    place = jnp.stack([y_hi, x]).astype(jnp.int32)
    table = jnp.concatenate([block_cols.reshape(-1), block_count, place])
    loss_here = ((y_lo * 2 + y_hi) * 4 + x == LOSS_ROW // PIECE).astype(jnp.int32).reshape(1)

    swap = [(0, 1), (1, 0)]
    both = lax.all_gather(features, "y_hi", axis=0, tiled=True)
    copies_of = [((4, 2 * own_rows, F), bf16)]
    (copies,) = call(copies_kernel, copies_of, [VMEM], [ANY], [pltpu.SemaphoreType.DMA((4,))])(both)
    feats_all = exchange(copies.reshape(8 * own_rows, F), "x")
    pad = ((0, 0), (0, CP - C))
    w_self_p, w_neigh_p = jnp.pad(w_self, pad), jnp.pad(w_neigh, pad)
    grads, keep, send, own = call(
        layer_kernel,
        [
            ((N_NEAR * PIECE, BS), bf16),
            ((8, CP, BS), f32),
            ((8, CP, BS), bf16),
            ((F, own_rows), f32),
        ],
        [SMEM] + [VMEM] * 7,
        scratch=[pltpu.VMEM((16, CP, BS), f32)],
    )(
        table, feats_all, features, w_self_p.T, w_neigh_p.T, w_self_p, block_values,
        jnp.broadcast_to(labels[None], (8, own_rows)),
    )

    came = lax.ppermute(send, "x", [(i, i ^ 1) for i in range(4)])
    keep, send = call(halve_kernel, [((4, CP, BS), f32), ((4, CP, BS), bf16)], [VMEM] * 2)(keep, came)
    came = second = lax.ppermute(send, "x", [(i, 3 - i) for i in range(4)])
    keep, send = call(halve_kernel, [((2, CP, BS), f32), ((2, CP, BS), bf16)], [VMEM] * 2)(keep, came)
    came = lax.ppermute(send, "y_hi", swap)
    (grad_features,) = call(features_kernel, [((own_rows, F), bf16)], [VMEM] * 4)(keep, came, own, w_neigh_p)

    pieces = exchange(grads, NEAR).reshape(N_NEAR, PIECE, BS)
    (pieces,) = call(piece_kernel, [((N_FAR, PIECE, BS), bf16)], [SMEM, VMEM, SMEM])(loss_here, pieces, loss_here)
    pieces = exchange(pieces.reshape(N_FAR * PIECE, BS), FAR).reshape(N_FAR, PIECE, BS)
    (pieces,) = call(piece_kernel, [((N_NEAR, PIECE, BS), bf16)], [SMEM, VMEM, ANY])(loss_here, pieces, second)
    pieces = exchange(pieces.reshape(N_NEAR * PIECE, BS), NEAR)
    loss, grad_self, grad_neigh = call(
        functools.partial(grads_kernel, nodes_all),
        [((1, 1), f32), ((C, F), f32), ((C, F), f32)],
        [VMEM],
        [SMEM, VMEM, VMEM],
    )(pieces)
    return (loss.reshape(()), grad_self.T, grad_neigh.T, grad_features)


def solution(mesh):
    fine = Mesh(mesh.devices.reshape(SIZES), AXES)
    return jax.shard_map(
        per_device,
        mesh=fine,
        in_specs=(P(AXES, None), P(), P(), P(AXES, None), P(AXES), P(AXES, None, None, None), P(AXES)),
        out_specs=(P(), P(), P(), P(AXES, None)),
        check_vma=False,
    )
```

```python
import functools

import jax
import jax.numpy as jnp
from jax import lax
from jax.experimental import pallas as pl
from jax.experimental.pallas import tpu as pltpu
from jax.sharding import Mesh, PartitionSpec as P

AXES = ("y_lo", "z", "core", "y_hi", "x")
SIZES = (4, 12, 2, 2, 4)
NEAR = ("y_lo", "y_hi", "x")
FAR = ("z", "core")
N_NEAR, N_FAR = 32, 24
BS = 128
F = 256
C = 172
CP = 176
PIECE = 24
LOSS_ROW = C
ANY = pl.BlockSpec(memory_space=pl.ANY)
SMEM = pl.BlockSpec(memory_space=pltpu.SMEM)
VMEM = pl.BlockSpec(memory_space=pltpu.VMEM)
PARAMS = pltpu.CompilerParams(vmem_limit_bytes=40 * 2**20)


def split_three(value):
    high = value.astype(jnp.bfloat16).astype(jnp.float32)
    rest = value - high
    mid = rest.astype(jnp.bfloat16).astype(jnp.float32)
    return high, mid, rest - mid


def put_copies(source, out, start, sems):
    rows = pl.ds(start, source.shape[0])
    copies = [pltpu.make_async_copy(source, out.at[i, rows], sems.at[i]) for i in range(out.shape[0])]
    for copy in copies:
        copy.start()
    for copy in copies:
        copy.wait()


def copies_kernel(source, out, sems):
    put_copies(source, out, 0, sems)


def layer_kernel(
    table, feats_all, feats, w_self_t, w_neigh_t, w_self, values, labels,
    grads, keep, send, own, terms,
):
    nblocks, slots = values.shape[0], values.shape[1]
    cols = [[table[b * slots + s] for s in range(slots)] for b in range(nblocks)]
    counts = [table[nblocks * slots + b] for b in range(nblocks)]
    my_half, my_x = table[nblocks * (slots + 1)], table[nblocks * (slots + 1) + 1]

    def home(col):
        return (col // 2) % 4, (col // 8) ^ my_half, col % 2

    def start_row(col):
        owner_x, _, second = home(col)
        return pl.multiple_of((owner_x * 4 + (col // 8) * 2 + second) * BS, BS)

    live = []
    degree_col, degree_row, summed = [], [], []
    for b in range(nblocks):
        row = []
        total = None
        for s in range(slots):
            used = jnp.where(s < counts[b], 1.0, 0.0).astype(jnp.float32)
            block = values[b, s] * jnp.full((BS, BS), used, jnp.float32).astype(jnp.bfloat16)
            row.append(block)
            wide = block.astype(jnp.float32)
            total = wide if total is None else total + wide
        live.append(row)
        degree = jnp.sum(total, axis=1, keepdims=True)
        degree_col.append(degree)
        degree_row.append(jnp.broadcast_to(degree, (BS, BS)).T[0:1, :])
        picked = jnp.concatenate(
            [feats_all[pl.ds(start_row(cols[b][s]), BS), :] for s in range(slots)], axis=0
        )
        summed.append(
            jnp.dot(jnp.concatenate(row, axis=1), picked, preferred_element_type=jnp.float32) / degree
        )
    aggregate = jnp.concatenate(summed, axis=0).astype(jnp.bfloat16)
    degrees = jnp.concatenate(degree_row, axis=1)
    own_feats = feats[...]
    nt = (((1,), (1,)), ((), ()))
    logits = lax.dot_general(
        w_self_t[...], own_feats, nt, preferred_element_type=jnp.float32
    ) + lax.dot_general(w_neigh_t[...], aggregate, nt, preferred_element_type=jnp.float32)
    classes = lax.broadcasted_iota(jnp.int32, logits.shape, 0)
    real = classes < C
    top = jnp.max(jnp.where(real, logits, -3.0e38), axis=0, keepdims=True)
    shifted = jnp.where(real, jnp.exp(jnp.where(real, logits - top, 0.0)), 0.0)
    total_exp = jnp.sum(shifted, axis=0, keepdims=True)
    target = classes == labels[0:1, :]
    picked_logit = jnp.sum(jnp.where(target, logits, 0.0), axis=0, keepdims=True)
    lse = jnp.log(total_exp) + top
    loss = jnp.sum(lse - picked_logit, axis=1, keepdims=True)
    dlogits = (shifted / total_exp - jnp.where(target, 1.0, 0.0)).astype(jnp.bfloat16)

    high, mid, low = split_three(loss)
    both = (own_feats, aggregate)
    rows = lax.broadcasted_iota(jnp.int32, (CP, BS), 0)
    wide = [jnp.dot(dlogits, side, preferred_element_type=jnp.float32) for side in both]
    for q in range(4):
        part = wide[q // 2][:, (q % 2) * BS : (q % 2 + 1) * BS]
        if q == 0:
            part = jnp.where(rows == LOSS_ROW, high, part)
            part = jnp.where(rows == LOSS_ROW + 1, mid, part)
            part = jnp.where(rows == LOSS_ROW + 2, low, part)
        grads[q * CP : (q + 1) * CP, :] = part.astype(jnp.bfloat16)
    pad = grads.shape[0] - 4 * CP
    grads[4 * CP :, :] = jnp.zeros((pad, BS), jnp.bfloat16)

    own[...] = jnp.dot(w_self[...], dlogits, preferred_element_type=jnp.float32)
    scaled = (dlogits.astype(jnp.float32) / degrees).astype(jnp.bfloat16)
    terms[...] = jnp.zeros_like(terms)
    for b in range(nblocks):
        mine = scaled[:, b * BS : (b + 1) * BS]
        terms_of = []
        for s in range(0, slots, 2):
            pair = jnp.concatenate(live[b][s : s + 2], axis=1)
            both_terms = jnp.dot(mine, pair, preferred_element_type=jnp.float32)
            terms_of += [both_terms[:, :BS], both_terms[:, BS:]]
        for s, term in enumerate(terms_of):
            owner_x, across, second = home(cols[b][s])
            delta = owner_x ^ my_x
            late = delta // 2
            early = (delta % 2) ^ late
            terms[early * 8 + late * 4 + across * 2 + second] += term
    keep[...] = terms[0:8]
    send[...] = terms[8:16].astype(jnp.bfloat16)


def halve_kernel(kept, came, keep, send):
    half = kept.shape[0] // 2
    keep[...] = kept[0:half] + came[0:half].astype(jnp.float32)
    send[...] = (kept[half:] + came[half:].astype(jnp.float32)).astype(jnp.bfloat16)


def spread(total, loss_here, out):
    rows = lax.broadcasted_iota(jnp.int32, total.shape, 0)
    here = LOSS_ROW % PIECE
    carries = (rows >= here) & (rows < here + 3)
    loss = jnp.sum(jnp.where(carries, total, 0.0), axis=0, keepdims=True)
    high, mid, low = split_three(loss)
    fixed = jnp.where(rows == here, high, jnp.where(rows == here + 1, mid, low))
    use = carries & (jnp.full(total.shape, loss_here[0], jnp.int32) == 1)
    out[...] = jnp.broadcast_to(jnp.where(use, fixed, total).astype(jnp.bfloat16)[None], out.shape)


def piece_kernel(loss_here, pieces, after, out):
    spread(jnp.sum(pieces[...].astype(jnp.float32), axis=0), loss_here, out)


def results_kernel(nodes_all, pieces, kept, came, own, w_neigh, loss, grad_self, grad_neigh, grad_features):
    for r in range(2):
        scattered = (kept[r] + came[r].astype(jnp.float32)).astype(jnp.bfloat16)
        total = own[:, r * BS : (r + 1) * BS] + jnp.dot(
            w_neigh[...], scattered, preferred_element_type=jnp.float32
        )
        grad_features[r * BS : (r + 1) * BS, :] = total.T.astype(jnp.bfloat16)
    factor = float(nodes_all) ** (-0.5)
    outs = (grad_self, grad_neigh)
    for q in range(4):
        part = pieces[q * CP : (q + 1) * CP, :].astype(jnp.float32)
        if q == 0:
            carried = part[LOSS_ROW - 4 : CP, :]
            rows = lax.broadcasted_iota(jnp.int32, carried.shape, 0)
            lanes = lax.broadcasted_iota(jnp.int32, carried.shape, 1)
            use = (rows >= 4) & (rows < 7) & (lanes == 0)
            loss[0, 0] = jnp.sum(jnp.where(use, carried, 0.0)) / nodes_all
        outs[q // 2][:, (q % 2) * BS : (q % 2 + 1) * BS] = part[:C] * factor


def call(kernel, outs, in_specs, out_specs=None, scratch=(), aliases=None):
    shapes = [jax.ShapeDtypeStruct(shape, dtype) for shape, dtype in outs]
    return pl.pallas_call(
        kernel,
        out_shape=shapes,
        in_specs=in_specs,
        out_specs=out_specs or [VMEM] * len(shapes),
        scratch_shapes=list(scratch),
        input_output_aliases=aliases or {},
        compiler_params=PARAMS,
    )


def exchange(rows, axes):
    return lax.all_to_all(rows, axes, 0, 0, tiled=True)


def per_device(features, w_self, w_neigh, block_cols, block_count, block_values, labels):
    bf16, f32 = jnp.bfloat16, jnp.float32
    own_rows = features.shape[0]
    nodes_all = own_rows * 768
    y_lo, y_hi, x = (lax.axis_index(a) for a in NEAR)
    place = jnp.stack([y_hi, x]).astype(jnp.int32)
    table = jnp.concatenate([block_cols.reshape(-1), block_count, place])
    loss_here = ((y_lo * 2 + y_hi) * 4 + x == LOSS_ROW // PIECE).astype(jnp.int32).reshape(1)

    swap = [(0, 1), (1, 0)]
    both = lax.all_gather(features, "y_hi", axis=0, tiled=True)
    copies_of = [((4, 2 * own_rows, F), bf16)]
    (copies,) = call(copies_kernel, copies_of, [VMEM], [ANY], [pltpu.SemaphoreType.DMA((4,))])(both)
    feats_all = exchange(copies.reshape(8 * own_rows, F), "x")
    pad = ((0, 0), (0, CP - C))
    w_self_p, w_neigh_p = jnp.pad(w_self, pad), jnp.pad(w_neigh, pad)
    grads, keep, send, own = call(
        layer_kernel,
        [
            ((N_NEAR * PIECE, BS), bf16),
            ((8, CP, BS), f32),
            ((8, CP, BS), bf16),
            ((F, own_rows), f32),
        ],
        [SMEM] + [VMEM] * 7,
        scratch=[pltpu.VMEM((16, CP, BS), f32)],
    )(
        table, feats_all, features, w_self_p.T, w_neigh_p.T, w_self_p, block_values,
        jnp.broadcast_to(labels[None], (8, own_rows)),
    )

    came = lax.ppermute(send, "x", [(i, i ^ 1) for i in range(4)])
    keep, send = call(halve_kernel, [((4, CP, BS), f32), ((4, CP, BS), bf16)], [VMEM] * 2)(keep, came)
    came = second = lax.ppermute(send, "x", [(i, 3 - i) for i in range(4)])
    keep, send = call(halve_kernel, [((2, CP, BS), f32), ((2, CP, BS), bf16)], [VMEM] * 2)(keep, came)
    came = lax.ppermute(send, "y_hi", swap)
    pieces = exchange(grads, NEAR).reshape(N_NEAR, PIECE, BS)
    (pieces,) = call(piece_kernel, [((N_FAR, PIECE, BS), bf16)], [SMEM, VMEM, SMEM])(loss_here, pieces, loss_here)
    pieces = exchange(pieces.reshape(N_FAR * PIECE, BS), FAR).reshape(N_FAR, PIECE, BS)
    (pieces,) = call(piece_kernel, [((N_NEAR, PIECE, BS), bf16)], [SMEM, VMEM, ANY])(loss_here, pieces, second)
    pieces = exchange(pieces.reshape(N_NEAR * PIECE, BS), NEAR)
    loss, grad_self, grad_neigh, grad_features = call(
        functools.partial(results_kernel, nodes_all),
        [((1, 1), f32), ((C, F), f32), ((C, F), f32), ((own_rows, F), bf16)],
        [VMEM] * 5,
        [SMEM, VMEM, VMEM, VMEM],
    )(pieces, keep, came, own, w_neigh_p)
    return (loss.reshape(()), grad_self.T, grad_neigh.T, grad_features)


def solution(mesh):
    fine = Mesh(mesh.devices.reshape(SIZES), AXES)
    return jax.shard_map(
        per_device,
        mesh=fine,
        in_specs=(P(AXES, None), P(), P(), P(AXES, None), P(AXES), P(AXES, None, None, None), P(AXES)),
        out_specs=(P(), P(), P(), P(AXES, None)),
        check_vma=False,
    )
```

```python
import functools

import jax
import jax.numpy as jnp
from jax import lax
from jax.experimental import pallas as pl
from jax.experimental.pallas import tpu as pltpu
from jax.sharding import Mesh, PartitionSpec as P

AXES = ("y_lo", "z", "core", "y_hi", "x")
SIZES = (4, 12, 2, 2, 4)
NEAR = ("x", "y_hi", "y_lo")
FAR = ("z", "core")
N_NEAR, N_FAR = 32, 24
BS = 128
F = 256
C = 172
CP = 176
PIECE = 24
LOSS_ROW = C
ANY = pl.BlockSpec(memory_space=pl.ANY)
SMEM = pl.BlockSpec(memory_space=pltpu.SMEM)
VMEM = pl.BlockSpec(memory_space=pltpu.VMEM)
PARAMS = pltpu.CompilerParams(vmem_limit_bytes=40 * 2**20)


def split_three(value):
    high = value.astype(jnp.bfloat16).astype(jnp.float32)
    rest = value - high
    mid = rest.astype(jnp.bfloat16).astype(jnp.float32)
    return high, mid, rest - mid


def put_copies(source, out, start, sems):
    rows = pl.ds(start, source.shape[0])
    copies = [pltpu.make_async_copy(source, out.at[i, rows], sems.at[i]) for i in range(out.shape[0])]
    for copy in copies:
        copy.start()
    for copy in copies:
        copy.wait()


def copies_kernel(source, out, sems):
    put_copies(source, out, 0, sems)


def layer_kernel(
    table, feats_all, feats, w_self_t, w_neigh_t, w_self, values, labels,
    grads, keep, send, own, terms,
):
    nblocks, slots = values.shape[0], values.shape[1]
    cols = [[table[b * slots + s] for s in range(slots)] for b in range(nblocks)]
    counts = [table[nblocks * slots + b] for b in range(nblocks)]
    my_half, my_x = table[nblocks * (slots + 1)], table[nblocks * (slots + 1) + 1]

    def home(col):
        return (col // 2) % 4, (col // 8) ^ my_half, col % 2

    def start_row(col):
        owner_x, _, second = home(col)
        return pl.multiple_of((owner_x * 4 + (col // 8) * 2 + second) * BS, BS)

    live = []
    degree_col, degree_row, summed = [], [], []
    for b in range(nblocks):
        row = []
        total = None
        for s in range(slots):
            used = jnp.where(s < counts[b], 1.0, 0.0).astype(jnp.float32)
            block = values[b, s] * jnp.full((BS, BS), used, jnp.float32).astype(jnp.bfloat16)
            row.append(block)
            wide = block.astype(jnp.float32)
            total = wide if total is None else total + wide
        live.append(row)
        degree = jnp.sum(total, axis=1, keepdims=True)
        degree_col.append(degree)
        degree_row.append(jnp.broadcast_to(degree, (BS, BS)).T[0:1, :])
        picked = jnp.concatenate(
            [feats_all[pl.ds(start_row(cols[b][s]), BS), :] for s in range(slots)], axis=0
        )
        summed.append(
            jnp.dot(jnp.concatenate(row, axis=1), picked, preferred_element_type=jnp.float32) / degree
        )
    aggregate = jnp.concatenate(summed, axis=0).astype(jnp.bfloat16)
    degrees = jnp.concatenate(degree_row, axis=1)
    own_feats = feats[...]
    nt = (((1,), (1,)), ((), ()))
    logits = lax.dot_general(
        w_self_t[...], own_feats, nt, preferred_element_type=jnp.float32
    ) + lax.dot_general(w_neigh_t[...], aggregate, nt, preferred_element_type=jnp.float32)
    classes = lax.broadcasted_iota(jnp.int32, logits.shape, 0)
    real = classes < C
    top = jnp.max(jnp.where(real, logits, -3.0e38), axis=0, keepdims=True)
    shifted = jnp.where(real, jnp.exp(jnp.where(real, logits - top, 0.0)), 0.0)
    total_exp = jnp.sum(shifted, axis=0, keepdims=True)
    target = classes == labels[0:1, :]
    picked_logit = jnp.sum(jnp.where(target, logits, 0.0), axis=0, keepdims=True)
    lse = jnp.log(total_exp) + top
    loss = jnp.sum(lse - picked_logit, axis=1, keepdims=True)
    dlogits = (shifted / total_exp - jnp.where(target, 1.0, 0.0)).astype(jnp.bfloat16)

    high, mid, low = split_three(loss)
    both = (own_feats, aggregate)
    rows = lax.broadcasted_iota(jnp.int32, (CP, BS), 0)
    wide = [jnp.dot(dlogits, side, preferred_element_type=jnp.float32) for side in both]
    for q in range(4):
        part = wide[q // 2][:, (q % 2) * BS : (q % 2 + 1) * BS]
        if q == 0:
            part = jnp.where(rows == LOSS_ROW, high, part)
            part = jnp.where(rows == LOSS_ROW + 1, mid, part)
            part = jnp.where(rows == LOSS_ROW + 2, low, part)
        grads[q * CP : (q + 1) * CP, :] = part.astype(jnp.bfloat16)
    pad = grads.shape[0] - 4 * CP
    grads[4 * CP :, :] = jnp.zeros((pad, BS), jnp.bfloat16)

    own[...] = jnp.dot(w_self[...], dlogits, preferred_element_type=jnp.float32)
    scaled = (dlogits.astype(jnp.float32) / degrees).astype(jnp.bfloat16)
    terms[...] = jnp.zeros_like(terms)
    for b in range(nblocks):
        mine = scaled[:, b * BS : (b + 1) * BS]
        terms_of = []
        for s in range(0, slots, 2):
            pair = jnp.concatenate(live[b][s : s + 2], axis=1)
            both_terms = jnp.dot(mine, pair, preferred_element_type=jnp.float32)
            terms_of += [both_terms[:, :BS], both_terms[:, BS:]]
        for s, term in enumerate(terms_of):
            owner_x, across, second = home(cols[b][s])
            delta = owner_x ^ my_x
            late = delta // 2
            early = (delta % 2) ^ late
            terms[early * 8 + late * 4 + across * 2 + second] += term
    keep[...] = terms[0:8]
    send[...] = terms[8:16].astype(jnp.bfloat16)


def halve_kernel(kept, came, keep, send):
    half = kept.shape[0] // 2
    keep[...] = kept[0:half] + came[0:half].astype(jnp.float32)
    send[...] = (kept[half:] + came[half:].astype(jnp.float32)).astype(jnp.bfloat16)


def spread(total, loss_here, out):
    rows = lax.broadcasted_iota(jnp.int32, total.shape, 0)
    here = LOSS_ROW % PIECE
    carries = (rows >= here) & (rows < here + 3)
    loss = jnp.sum(jnp.where(carries, total, 0.0), axis=0, keepdims=True)
    high, mid, low = split_three(loss)
    fixed = jnp.where(rows == here, high, jnp.where(rows == here + 1, mid, low))
    use = carries & (jnp.full(total.shape, loss_here[0], jnp.int32) == 1)
    out[...] = jnp.broadcast_to(jnp.where(use, fixed, total).astype(jnp.bfloat16)[None], out.shape)


def piece_kernel(loss_here, pieces, after, out):
    spread(jnp.sum(pieces[...].astype(jnp.float32), axis=0), loss_here, out)


def results_kernel(nodes_all, pieces, kept, came, own, w_neigh, loss, grad_self, grad_neigh, grad_features):
    for r in range(2):
        scattered = (kept[r] + came[r].astype(jnp.float32)).astype(jnp.bfloat16)
        total = own[:, r * BS : (r + 1) * BS] + jnp.dot(
            w_neigh[...], scattered, preferred_element_type=jnp.float32
        )
        grad_features[r * BS : (r + 1) * BS, :] = total.T.astype(jnp.bfloat16)
    factor = float(nodes_all) ** (-0.5)
    outs = (grad_self, grad_neigh)
    for q in range(4):
        part = pieces[q * CP : (q + 1) * CP, :].astype(jnp.float32)
        if q == 0:
            carried = part[LOSS_ROW - 4 : CP, :]
            rows = lax.broadcasted_iota(jnp.int32, carried.shape, 0)
            lanes = lax.broadcasted_iota(jnp.int32, carried.shape, 1)
            use = (rows >= 4) & (rows < 7) & (lanes == 0)
            loss[0, 0] = jnp.sum(jnp.where(use, carried, 0.0)) / nodes_all
        outs[q // 2][:, (q % 2) * BS : (q % 2 + 1) * BS] = part[:C] * factor


def call(kernel, outs, in_specs, out_specs=None, scratch=(), aliases=None):
    shapes = [jax.ShapeDtypeStruct(shape, dtype) for shape, dtype in outs]
    return pl.pallas_call(
        kernel,
        out_shape=shapes,
        in_specs=in_specs,
        out_specs=out_specs or [VMEM] * len(shapes),
        scratch_shapes=list(scratch),
        input_output_aliases=aliases or {},
        compiler_params=PARAMS,
    )


def exchange(rows, axes):
    return lax.all_to_all(rows, axes, 0, 0, tiled=True)


def per_device(features, w_self, w_neigh, block_cols, block_count, block_values, labels):
    bf16, f32 = jnp.bfloat16, jnp.float32
    own_rows = features.shape[0]
    nodes_all = own_rows * 768
    x, y_hi, y_lo = (lax.axis_index(a) for a in NEAR)
    place = jnp.stack([y_hi, x]).astype(jnp.int32)
    table = jnp.concatenate([block_cols.reshape(-1), block_count, place])
    loss_here = ((x * 2 + y_hi) * 4 + y_lo == LOSS_ROW // PIECE).astype(jnp.int32).reshape(1)

    swap = [(0, 1), (1, 0)]
    both = lax.all_gather(features, "y_hi", axis=0, tiled=True)
    copies_of = [((4, 2 * own_rows, F), bf16)]
    (copies,) = call(copies_kernel, copies_of, [VMEM], [ANY], [pltpu.SemaphoreType.DMA((4,))])(both)
    feats_all = exchange(copies.reshape(8 * own_rows, F), "x")
    pad = ((0, 0), (0, CP - C))
    w_self_p, w_neigh_p = jnp.pad(w_self, pad), jnp.pad(w_neigh, pad)
    grads, keep, send, own = call(
        layer_kernel,
        [
            ((N_NEAR * PIECE, BS), bf16),
            ((8, CP, BS), f32),
            ((8, CP, BS), bf16),
            ((F, own_rows), f32),
        ],
        [SMEM] + [VMEM] * 7,
        scratch=[pltpu.VMEM((16, CP, BS), f32)],
    )(
        table, feats_all, features, w_self_p.T, w_neigh_p.T, w_self_p, block_values,
        jnp.broadcast_to(labels[None], (8, own_rows)),
    )

    came = lax.ppermute(send, "x", [(i, i ^ 1) for i in range(4)])
    keep, send = call(halve_kernel, [((4, CP, BS), f32), ((4, CP, BS), bf16)], [VMEM] * 2)(keep, came)
    came = second = lax.ppermute(send, "x", [(i, 3 - i) for i in range(4)])
    keep, send = call(halve_kernel, [((2, CP, BS), f32), ((2, CP, BS), bf16)], [VMEM] * 2)(keep, came)
    came = lax.ppermute(send, "y_hi", swap)
    pieces = exchange(grads, NEAR).reshape(N_NEAR, PIECE, BS)
    (pieces,) = call(piece_kernel, [((N_FAR, PIECE, BS), bf16)], [SMEM, VMEM, SMEM])(loss_here, pieces, loss_here)
    pieces = exchange(pieces.reshape(N_FAR * PIECE, BS), FAR).reshape(N_FAR, PIECE, BS)
    (pieces,) = call(piece_kernel, [((N_NEAR, PIECE, BS), bf16)], [SMEM, VMEM, ANY])(loss_here, pieces, second)
    pieces = exchange(pieces.reshape(N_NEAR * PIECE, BS), NEAR)
    loss, grad_self, grad_neigh, grad_features = call(
        functools.partial(results_kernel, nodes_all),
        [((1, 1), f32), ((C, F), f32), ((C, F), f32), ((own_rows, F), bf16)],
        [VMEM] * 5,
        [SMEM, VMEM, VMEM, VMEM],
    )(pieces, keep, came, own, w_neigh_p)
    return (loss.reshape(()), grad_self.T, grad_neigh.T, grad_features)


def solution(mesh):
    fine = Mesh(mesh.devices.reshape(SIZES), AXES)
    return jax.shard_map(
        per_device,
        mesh=fine,
        in_specs=(P(AXES, None), P(), P(), P(AXES, None), P(AXES), P(AXES, None, None, None), P(AXES)),
        out_specs=(P(), P(), P(), P(AXES, None)),
        check_vma=False,
    )
```

```python
import functools

import jax
import jax.numpy as jnp
from jax import lax
from jax.experimental import pallas as pl
from jax.experimental.pallas import tpu as pltpu
from jax.sharding import Mesh, PartitionSpec as P

AXES = ("y_lo", "z", "core", "y_hi", "x")
SIZES = (4, 12, 2, 2, 4)
NEAR = ("x", "y_hi", "y_lo")
FAR = ("z", "core")
N_NEAR, N_FAR = 32, 24
BS = 128
F = 256
C = 172
CP = 176
PIECE = 24
LOSS_ROW = C
ANY = pl.BlockSpec(memory_space=pl.ANY)
SMEM = pl.BlockSpec(memory_space=pltpu.SMEM)
VMEM = pl.BlockSpec(memory_space=pltpu.VMEM)
PARAMS = pltpu.CompilerParams(vmem_limit_bytes=40 * 2**20)


def split_three(value):
    high = value.astype(jnp.bfloat16).astype(jnp.float32)
    rest = value - high
    mid = rest.astype(jnp.bfloat16).astype(jnp.float32)
    return high, mid, rest - mid


def put_copies(source, out, start, sems):
    rows = pl.ds(start, source.shape[0])
    copies = [pltpu.make_async_copy(source, out.at[i, rows], sems.at[i]) for i in range(out.shape[0])]
    for copy in copies:
        copy.start()
    for copy in copies:
        copy.wait()


def copies_kernel(source, out, sems):
    put_copies(source, out, 0, sems)


def layer_kernel(
    table, feats_all, feats, w_self_t, w_neigh_t, w_self, values, labels,
    grads, keep, send, own, terms,
):
    nblocks, slots = values.shape[0], values.shape[1]
    cols = [[table[b * slots + s] for s in range(slots)] for b in range(nblocks)]
    counts = [table[nblocks * slots + b] for b in range(nblocks)]
    my_half, my_x = table[nblocks * (slots + 1)], table[nblocks * (slots + 1) + 1]

    def home(col):
        return (col // 2) % 4, (col // 8) ^ my_half, col % 2

    def start_row(col):
        owner_x, _, second = home(col)
        return pl.multiple_of((owner_x * 4 + (col // 8) * 2 + second) * BS, BS)

    live = []
    degree_col, summed = [], []
    for b in range(nblocks):
        row = []
        total = None
        for s in range(slots):
            used = jnp.where(s < counts[b], 1.0, 0.0).astype(jnp.float32)
            block = values[b, s] * jnp.full((BS, BS), used, jnp.float32).astype(jnp.bfloat16)
            row.append(block)
            wide = block.astype(jnp.float32)
            total = wide if total is None else total + wide
        live.append(row)
        degree = jnp.sum(total, axis=1, keepdims=True)
        degree_col.append(degree)
        picked = jnp.concatenate(
            [feats_all[pl.ds(start_row(cols[b][s]), BS), :] for s in range(slots)], axis=0
        )
        summed.append(
            jnp.dot(jnp.concatenate(row, axis=1), picked, preferred_element_type=jnp.float32) / degree
        )
    aggregate = jnp.concatenate(summed, axis=0).astype(jnp.bfloat16)
    lanes = lax.broadcasted_iota(jnp.int32, (BS, BS), 1)
    turned = jnp.where(lanes == 0, degree_col[0], degree_col[1]).T
    degrees = jnp.concatenate([turned[0:1, :], turned[1:2, :]], axis=1)
    own_feats = feats[...]
    nt = (((1,), (1,)), ((), ()))
    logits = lax.dot_general(
        w_self_t[...], own_feats, nt, preferred_element_type=jnp.float32
    ) + lax.dot_general(w_neigh_t[...], aggregate, nt, preferred_element_type=jnp.float32)
    classes = lax.broadcasted_iota(jnp.int32, logits.shape, 0)
    real = classes < C
    top = jnp.max(jnp.where(real, logits, -3.0e38), axis=0, keepdims=True)
    shifted = jnp.where(real, jnp.exp(logits - top), 0.0)
    total_exp = jnp.sum(shifted, axis=0, keepdims=True)
    target = classes == labels[0:1, :]
    picked_logit = jnp.sum(jnp.where(target, logits, 0.0), axis=0, keepdims=True)
    lse = jnp.log(total_exp) + top
    loss = jnp.sum(lse - picked_logit, axis=1, keepdims=True)
    dlogits = (shifted / total_exp - jnp.where(target, 1.0, 0.0)).astype(jnp.bfloat16)

    high, mid, low = split_three(loss)
    both = (own_feats, aggregate)
    rows = lax.broadcasted_iota(jnp.int32, (CP, BS), 0)
    wide = [jnp.dot(dlogits, side, preferred_element_type=jnp.float32) for side in both]
    for q in range(4):
        part = wide[q // 2][:, (q % 2) * BS : (q % 2 + 1) * BS]
        if q == 0:
            part = jnp.where(rows == LOSS_ROW, high, part)
            part = jnp.where(rows == LOSS_ROW + 1, mid, part)
            part = jnp.where(rows == LOSS_ROW + 2, low, part)
        grads[q * CP : (q + 1) * CP, :] = part.astype(jnp.bfloat16)
    pad = grads.shape[0] - 4 * CP
    grads[4 * CP :, :] = jnp.zeros((pad, BS), jnp.bfloat16)

    own[...] = jnp.dot(w_self[...], dlogits, preferred_element_type=jnp.float32)
    scaled = (dlogits.astype(jnp.float32) / degrees).astype(jnp.bfloat16)
    terms[...] = jnp.zeros_like(terms)
    for b in range(nblocks):
        mine = scaled[:, b * BS : (b + 1) * BS]
        terms_of = []
        for s in range(0, slots, 2):
            pair = jnp.concatenate(live[b][s : s + 2], axis=1)
            both_terms = jnp.dot(mine, pair, preferred_element_type=jnp.float32)
            terms_of += [both_terms[:, :BS], both_terms[:, BS:]]
        for s, term in enumerate(terms_of):
            owner_x, across, second = home(cols[b][s])
            delta = owner_x ^ my_x
            late = delta // 2
            early = (delta % 2) ^ late
            terms[early * 8 + late * 4 + across * 2 + second] += term
    keep[...] = terms[0:8]
    send[...] = terms[8:16].astype(jnp.bfloat16)


def halve_kernel(kept, came, keep, send):
    half = kept.shape[0] // 2
    keep[...] = kept[0:half] + came[0:half].astype(jnp.float32)
    send[...] = (kept[half:] + came[half:].astype(jnp.float32)).astype(jnp.bfloat16)


def spread(total, loss_here, out):
    rows = lax.broadcasted_iota(jnp.int32, total.shape, 0)
    here = LOSS_ROW % PIECE
    carries = (rows >= here) & (rows < here + 3)
    loss = jnp.sum(jnp.where(carries, total, 0.0), axis=0, keepdims=True)
    high, mid, low = split_three(loss)
    fixed = jnp.where(rows == here, high, jnp.where(rows == here + 1, mid, low))
    use = carries & (jnp.full(total.shape, loss_here[0], jnp.int32) == 1)
    out[...] = jnp.broadcast_to(jnp.where(use, fixed, total).astype(jnp.bfloat16)[None], out.shape)


def piece_kernel(loss_here, pieces, after, out):
    spread(jnp.sum(pieces[...].astype(jnp.float32), axis=0), loss_here, out)


def results_kernel(nodes_all, pieces, kept, came, own, w_neigh, loss, grad_self, grad_neigh, grad_features):
    for r in range(2):
        scattered = (kept[r] + came[r].astype(jnp.float32)).astype(jnp.bfloat16)
        total = own[:, r * BS : (r + 1) * BS] + jnp.dot(
            w_neigh[...], scattered, preferred_element_type=jnp.float32
        )
        grad_features[r * BS : (r + 1) * BS, :] = total.T.astype(jnp.bfloat16)
    factor = float(nodes_all) ** (-0.5)
    outs = (grad_self, grad_neigh)
    for q in range(4):
        part = pieces[q * CP : (q + 1) * CP, :].astype(jnp.float32)
        if q == 0:
            carried = part[LOSS_ROW - 4 : CP, :]
            rows = lax.broadcasted_iota(jnp.int32, carried.shape, 0)
            lanes = lax.broadcasted_iota(jnp.int32, carried.shape, 1)
            use = (rows >= 4) & (rows < 7) & (lanes == 0)
            loss[0, 0] = jnp.sum(jnp.where(use, carried, 0.0)) / nodes_all
        outs[q // 2][:, (q % 2) * BS : (q % 2 + 1) * BS] = part[:C] * factor


def call(kernel, outs, in_specs, out_specs=None, scratch=(), aliases=None):
    shapes = [jax.ShapeDtypeStruct(shape, dtype) for shape, dtype in outs]
    return pl.pallas_call(
        kernel,
        out_shape=shapes,
        in_specs=in_specs,
        out_specs=out_specs or [VMEM] * len(shapes),
        scratch_shapes=list(scratch),
        input_output_aliases=aliases or {},
        compiler_params=PARAMS,
    )


def exchange(rows, axes):
    return lax.all_to_all(rows, axes, 0, 0, tiled=True)


def per_device(features, w_self, w_neigh, block_cols, block_count, block_values, labels):
    bf16, f32 = jnp.bfloat16, jnp.float32
    own_rows = features.shape[0]
    nodes_all = own_rows * 768
    x, y_hi, y_lo = (lax.axis_index(a) for a in NEAR)
    place = jnp.stack([y_hi, x]).astype(jnp.int32)
    table = jnp.concatenate([block_cols.reshape(-1), block_count, place])
    loss_here = ((x * 2 + y_hi) * 4 + y_lo == LOSS_ROW // PIECE).astype(jnp.int32).reshape(1)

    swap = [(0, 1), (1, 0)]
    both = lax.all_gather(features, "y_hi", axis=0, tiled=True)
    copies_of = [((4, 2 * own_rows, F), bf16)]
    (copies,) = call(copies_kernel, copies_of, [VMEM], [ANY], [pltpu.SemaphoreType.DMA((4,))])(both)
    feats_all = exchange(copies.reshape(8 * own_rows, F), "x")
    pad = ((0, 0), (0, CP - C))
    w_self_p, w_neigh_p = jnp.pad(w_self, pad), jnp.pad(w_neigh, pad)
    grads, keep, send, own = call(
        layer_kernel,
        [
            ((N_NEAR * PIECE, BS), bf16),
            ((8, CP, BS), f32),
            ((8, CP, BS), bf16),
            ((F, own_rows), f32),
        ],
        [SMEM] + [VMEM] * 7,
        scratch=[pltpu.VMEM((16, CP, BS), f32)],
    )(
        table, feats_all, features, w_self_p.T, w_neigh_p.T, w_self_p, block_values,
        jnp.broadcast_to(labels[None], (8, own_rows)),
    )

    came = lax.ppermute(send, "x", [(i, i ^ 1) for i in range(4)])
    keep, send = call(halve_kernel, [((4, CP, BS), f32), ((4, CP, BS), bf16)], [VMEM] * 2)(keep, came)
    came = second = lax.ppermute(send, "x", [(i, 3 - i) for i in range(4)])
    keep, send = call(halve_kernel, [((2, CP, BS), f32), ((2, CP, BS), bf16)], [VMEM] * 2)(keep, came)
    came = lax.ppermute(send, "y_hi", swap)
    pieces = exchange(grads, NEAR).reshape(N_NEAR, PIECE, BS)
    (pieces,) = call(piece_kernel, [((N_FAR, PIECE, BS), bf16)], [SMEM, VMEM, SMEM])(loss_here, pieces, loss_here)
    pieces = exchange(pieces.reshape(N_FAR * PIECE, BS), FAR).reshape(N_FAR, PIECE, BS)
    (pieces,) = call(piece_kernel, [((N_NEAR, PIECE, BS), bf16)], [SMEM, VMEM, ANY])(loss_here, pieces, second)
    pieces = exchange(pieces.reshape(N_NEAR * PIECE, BS), NEAR)
    loss, grad_self, grad_neigh, grad_features = call(
        functools.partial(results_kernel, nodes_all),
        [((1, 1), f32), ((C, F), f32), ((C, F), f32), ((own_rows, F), bf16)],
        [VMEM] * 5,
        [SMEM, VMEM, VMEM, VMEM],
    )(pieces, keep, came, own, w_neigh_p)
    return (loss.reshape(()), grad_self.T, grad_neigh.T, grad_features)


def solution(mesh):
    fine = Mesh(mesh.devices.reshape(SIZES), AXES)
    return jax.shard_map(
        per_device,
        mesh=fine,
        in_specs=(P(AXES, None), P(), P(), P(AXES, None), P(AXES), P(AXES, None, None, None), P(AXES)),
        out_specs=(P(), P(), P(), P(AXES, None)),
        check_vma=False,
    )
```
